32 devices in a mesh: row: 4 (over x, core), col: 4 (over z), depth: 2 (over y).
Axes of the slice: x: 2, y: 2, z: 4, core: 2. Of those that a mesh axis runs over, the one named last changes fastest.
Arguments:
- normed: bfloat16 [1024, 3072], P(('depth', 'row'), 'col'), may hold values from -6 to 6
- up_weight: bfloat16 [3072, 12288], P('col', 'row'), may hold values from -0.109375 to 0.109375
- down_weight: bfloat16 [12288, 3072], P('row', 'col'), may hold values from -0.0546875 to 0.0546875
- out_grad: bfloat16 [1024, 3072], P(('depth', 'row'), 'col'), may hold values from -6 to 6
Outputs:
- branch_out: bfloat16 [1024, 3072], P(('depth', 'row'), 'col')
- normed_grad: bfloat16 [1024, 3072], P(('depth', 'row'), 'col')
- up_grad: float32 [3072, 12288], P(('col', 'depth'), 'row')
- down_grad: float32 [12288, 3072], P(('row', 'depth'), 'col')
The draws below stay inside these ranges and needn't reach their ends.
All inputs are finite; a program needn't handle non-finite values.
Results may differ from the reference program's by a relative error of at most 0.029.
Values may be sent and summed in bfloat16 or wider, within the bound.
No kernel may reach another device: no remote copies, remote signals or barrier semaphores. Data moves between devices by JAX's collectives and lax.ppermute only.
A program may use at most 64 MiB of HBM per device.

```python
import math
import jax
import jax.numpy as jnp
from jax import lax

D = 3072
F = 12288
TOKENS = 1024
N_ROW = 4
N_COL = 4
N_DEPTH = 2


def steps_of(stream_key, extent, pieces, least, top_value):
    def one(dim, blocks):
        heights = jax.random.uniform(jax.random.fold_in(jax.random.fold_in(stream_key, 6), dim), (blocks,), jnp.float32, least / len(pieces), top_value / len(pieces))
        return jnp.repeat(jnp.exp(heights), extent[dim] // blocks).reshape((-1,) + (1,) * (len(extent) - dim - 1))

    gain = one(*pieces[0])
    for cut in pieces[1:]:
        gain = gain * one(*cut)
    return gain


def centred(stream_key, extent, deviation, bound, cuts=(), kind=jnp.bfloat16):
    array = deviation * jax.random.normal(stream_key, extent, jnp.float32)
    if cuts:
        array = array * steps_of(stream_key, extent, cuts, -0.22, 0.18)
    return jnp.clip(array, -bound, bound).astype(kind)


def setup_inputs(seed: int = 0) -> dict:
    arg_keys = jax.random.split(jax.random.key(seed), 5)
    normed = centred(arg_keys[0], (TOKENS, D), 1.0, 6.0, ((0, 8), (1, 4)))
    up_weight = centred(arg_keys[1], (D, F), D ** -0.5, 0.109375, ((0, 4), (1, 4)))
    down_weight = centred(arg_keys[2], (F, D), F ** -0.5, 0.0546875, ((0, 4), (1, 4)))
    out_grad = centred(arg_keys[3], (TOKENS, D), 1.0, 6.0, ((0, 8), (1, 4)))
    return dict(normed=normed, up_weight=up_weight, down_weight=down_weight, out_grad=out_grad)


def rounded(value):
    return lax.optimization_barrier(value.astype(jnp.bfloat16)).astype(jnp.float32)

def gelu_parts(value):
    coeff = math.sqrt(2.0 / math.pi)
    inner = coeff * (value + 0.044715 * value * value * value)
    tangent = jnp.tanh(inner)
    activated = 0.5 * value * (1.0 + tangent)
    slope = 0.5 * (1.0 + tangent) + 0.5 * value * (1.0 - tangent * tangent) * coeff * (1.0 + 3.0 * 0.044715 * value * value)
    return (activated, slope)

def reference(normed, up_weight, down_weight, out_grad):
    col_width = D // N_COL
    row_width = F // N_ROW
    layer_rows = TOKENS // N_DEPTH
    pre_act = jnp.zeros((TOKENS, F), jnp.float32)
    back_act = jnp.zeros((TOKENS, F), jnp.float32)
    for block in range(N_COL):
        lower = block * col_width
        upper = lower + col_width
        pre_act = pre_act + rounded(jnp.dot(normed[:, lower:upper], up_weight[lower:upper, :], preferred_element_type=jnp.float32))
        back_act = back_act + rounded(jnp.dot(out_grad[:, lower:upper], down_weight[:, lower:upper].T, preferred_element_type=jnp.float32))
    active_full, slope = gelu_parts(pre_act)
    activated = active_full.astype(jnp.bfloat16)
    pre_grad = (back_act * slope).astype(jnp.bfloat16)
    branch_out = jnp.zeros((TOKENS, D), jnp.float32)
    normed_grad = jnp.zeros((TOKENS, D), jnp.float32)
    for block in range(N_ROW):
        lower = block * row_width
        upper = lower + row_width
        branch_out = branch_out + rounded(jnp.dot(activated[:, lower:upper], down_weight[lower:upper, :], preferred_element_type=jnp.float32))
        normed_grad = normed_grad + rounded(jnp.dot(pre_grad[:, lower:upper], up_weight[:, lower:upper].T, preferred_element_type=jnp.float32))
    up_grad = jnp.zeros((D, F), jnp.float32)
    down_grad = jnp.zeros((F, D), jnp.float32)
    for layer in range(N_DEPTH):
        lower = layer * layer_rows
        upper = lower + layer_rows
        up_grad = up_grad + rounded(jnp.dot(normed[lower:upper].T, pre_grad[lower:upper], preferred_element_type=jnp.float32))
        down_grad = down_grad + rounded(jnp.dot(activated[lower:upper].T, out_grad[lower:upper], preferred_element_type=jnp.float32))
    factor = 1.0 / math.sqrt(TOKENS)
    return (branch_out.astype(jnp.bfloat16), normed_grad.astype(jnp.bfloat16), up_grad * factor, down_grad * factor)
```

```python
import math

import jax
import jax.numpy as jnp
from jax import lax
from jax.experimental import pallas as pl
from jax.experimental.pallas import tpu as pltpu
from jax.sharding import PartitionSpec as P

F_PHASES = 3
STREAMS = 2
ROWS = 32


def gelu_parts(value):
    coeff = math.sqrt(2.0 / math.pi)
    inner = coeff * (value + 0.044715 * value * value * value)
    tangent = jnp.tanh(inner)
    activated = 0.5 * value * (1.0 + tangent)
    slope = 0.5 * (1.0 + tangent) + 0.5 * value * (1.0 - tangent * tangent) * coeff * (
        1.0 + 3.0 * 0.044715 * value * value
    )
    return (activated, slope)


def dot(left, right, left_dim, right_dim):
    return lax.dot_general(
        left, right, (((left_dim,), (right_dim,)), ((), ())), preferred_element_type=jnp.float32
    )


def to_bf16(value):
    return value.astype(jnp.bfloat16)


def to_f32(value):
    return value.astype(jnp.float32)


def cut_at(array, start, size, dim):
    starts, sizes = [0] * array.ndim, list(array.shape)
    starts[dim], sizes[dim] = start, size
    return lax.dynamic_slice(array, starts, sizes, allow_negative_indices=False)


def put_at(array, part, start, dim):
    starts = [0] * array.ndim
    starts[dim] = start
    return lax.dynamic_update_slice(array, part, starts, allow_negative_indices=False)


def swap(value, axis, mask):
    size = lax.axis_size(axis)
    return lax.ppermute(value, axis, [(i, i ^ mask) for i in range(size)])


def bits(size):
    return [1 << b for b in range(size.bit_length() - 1)]


def by_rows(count, body):
    def step(index, carry):
        body(pl.ds(pl.multiple_of(index * ROWS, ROWS), ROWS))
        return carry

    lax.fori_loop(0, count // ROWS, step, 0)


def bf16_array(*shape):
    return jax.ShapeDtypeStruct(shape, jnp.bfloat16)


def f32_array(*shape):
    return jax.ShapeDtypeStruct(shape, jnp.float32)


NO_COST = pl.CostEstimate(flops=1, bytes_accessed=1, transcendentals=0)
IN_VMEM = pl.BlockSpec(memory_space=pltpu.VMEM)
IN_SMEM = pl.BlockSpec(memory_space=pltpu.SMEM)


def local_kernel(body, out_shapes, scalar, operands, limit=8):
    scalars = [] if scalar is None else [scalar]
    return pl.pallas_call(
        body,
        out_shape=out_shapes,
        in_specs=[IN_SMEM] * len(scalars) + [IN_VMEM] * len(operands),
        out_specs=[IN_VMEM] * len(out_shapes),
        compiler_params=pltpu.CompilerParams(vmem_limit_bytes=limit * 2**20),
        cost_estimate=NO_COST,
    )(*scalars, *operands)


def spans(blocks):
    result, start = [], 0
    for block in blocks:
        result.append((block, start, start + block.shape[1]))
        start += block.shape[1]
    return result


def partials(start, blocks, up, down, half):
    count = sum(block.shape[1] for block in blocks)

    def body(*refs):
        *block_refs, up_ref, down_ref, out_ref = refs
        for k in range(2):
            at = slice(start + k * half, start + (k + 1) * half)
            for block, first, end in spans(block_refs):
                out_ref[k, 0, first:end] = to_bf16(dot(block[0], up_ref[:, at], 1, 0))
                out_ref[k, 1, first:end] = to_bf16(dot(block[1], down_ref[at, :], 1, 1))

    if half % 128:
        part = jnp.concatenate(blocks, axis=1)
        cut = [slice(start + k * half, start + (k + 1) * half) for k in range(2)]
        return to_bf16(
            jnp.stack(
                [
                    jnp.stack([dot(part[0], up[:, at], 1, 0), dot(part[1], down[at], 1, 1)])
                    for at in cut
                ]
            )
        )
    return local_kernel(body, [bf16_array(2, 2, count, half)], None, [*blocks, up, down])[0]


COPIES = 4


def load(column, up_weight, down_weight, start, size, limit):
    features = up_weight.shape[0]
    rows, part = features // COPIES, size // COPIES

    def body(column_ref, up_hbm, down_hbm, up_ref, down_ref, done):
        first = pl.multiple_of(column_ref[0] + start, size)
        copies = []
        for k in range(COPIES):
            at = pl.ds(k * rows, rows)
            copies.append((up_hbm.at[at, pl.ds(first, size)], up_ref.at[at, :]))
            there = pl.ds(pl.multiple_of(first + k * part, part), part)
            copies.append((down_hbm.at[there, :], down_ref.at[pl.ds(k * part, part), :]))
        copies = [
            pltpu.make_async_copy(source, target, done.at[k])
            for k, (source, target) in enumerate(copies)
        ]
        for copy in copies:
            copy.start()
        for copy in copies:
            copy.wait()

    in_place = pl.BlockSpec(memory_space=pl.ANY)
    return pl.pallas_call(
        body,
        out_shape=[bf16_array(features, size), bf16_array(size, features)],
        in_specs=[IN_SMEM, in_place, in_place],
        out_specs=[IN_VMEM] * 2,
        scratch_shapes=[pltpu.SemaphoreType.DMA((2 * COPIES,))],
        compiler_params=pltpu.CompilerParams(vmem_limit_bytes=limit * 2**20),
        cost_estimate=NO_COST,
    )(column, up_weight, down_weight)


def outputs_of(start, done, up, down, so_far, sizes):
    half, features = done.shape[3], up.shape[0]

    def total(done, up, down, before):
        value = list(before)
        for k in range(2):
            at = slice(start + k * half, start + (k + 1) * half)
            value[0] = value[0] + dot(done[k, 0], down[at, :], 1, 0)
            value[1] = value[1] + dot(done[k, 1], up[:, at], 1, 1)
        return value

    def body(done_ref, up_ref, down_ref, *refs):
        outs = refs[-len(sizes) :]
        befores = refs[: -len(sizes)]
        for kind, value in enumerate(total(done_ref, up_ref, down_ref, (0.0, 0.0))):
            first = 0
            for place, size in enumerate(sizes):
                part = value[first : first + size]
                if befores:
                    part = part + to_f32(befores[place][kind])
                outs[place][kind] = to_bf16(part)
                first += size

    if half % 128:
        before = (0.0, 0.0)
        if so_far:
            before = to_f32(jnp.concatenate(so_far, axis=1))
        value = to_bf16(jnp.stack(total(done, up, down, before)))
        return jnp.split(value, [sum(sizes[:k]) for k in range(1, len(sizes))], axis=1)
    shapes = [bf16_array(2, size, features) for size in sizes]
    return local_kernel(body, shapes, None, [done, up, down, *so_far])


def sum_of(blocks):
    if len(blocks) == 1:
        return blocks[0]

    def body(*refs):
        def rows(at):
            for kind in range(2):
                total = to_f32(refs[0][kind, at, :])
                for ref in refs[1:-1]:
                    total = total + to_f32(ref[kind, at, :])
                refs[-1][kind, at, :] = to_bf16(total)

        by_rows(blocks[0].shape[1], rows)

    return local_kernel(body, [bf16_array(*blocks[0].shape)], None, blocks)[0]


def gradient(kind, so_far, done, parts):
    half, features = done[0].shape[3], parts[0][0].shape[2]
    pairs = len(done)
    if half % 128:
        total = 0.0 if so_far is None else so_far
        for value, blocks in zip(done, parts):
            both = jnp.concatenate([value[0, kind], value[1, kind]], axis=-1)
            block = jnp.concatenate(blocks, axis=1)[1 - kind]
            total = total + (dot(block, both, 0, 0) if kind else dot(both, block, 0, 0))
        return total

    def body(*refs):
        done_refs, block_refs, out_ref = refs[:pairs], list(refs[pairs:-1]), refs[-1]
        part_refs = [[block_refs.pop(0) for _ in blocks] for blocks in parts]
        for k in range(2):
            at = slice(k * half, (k + 1) * half)
            total = 0.0
            if so_far is not None:
                total = block_refs[0][:, at] if kind else block_refs[0][at, :]
            for done_ref, blocks in zip(done_refs, part_refs):
                for block, first, end in spans(blocks):
                    value = done_ref[k, kind, first:end]
                    if kind:
                        total = total + dot(block[0], value, 0, 0)
                    else:
                        total = total + dot(value, block[1], 0, 0)
            if kind:
                out_ref[:, at] = total
            else:
                out_ref[at, :] = total

    shape = f32_array(features, 2 * half) if kind else f32_array(2 * half, features)
    operands = [*done, *(block for blocks in parts for block in blocks)]
    operands += [] if so_far is None else [so_far]
    return local_kernel(body, [shape], None, operands, 12)[0]


def up_rows(row, size, sums, done, parts, kind):
    half = sums.shape[1] // 2
    if half % 128:
        total = cut_at(sums, row[0], size, 0)
        for value, blocks in zip(done, parts):
            tokens = cut_at(jnp.concatenate(blocks, axis=1)[0], row[0], size, 1)
            total = total + dot(tokens, jnp.concatenate([value[0, 1], value[1, 1]], axis=-1), 0, 0)
        return total.astype(kind)

    def body(row_ref, sums_ref, *refs):
        at = pl.ds(pl.multiple_of(row_ref[0], size), size)
        out_ref, done_refs = refs[-1], refs[: len(done)]
        block_refs = list(refs[len(done) : -1])
        part_refs = [[block_refs.pop(0) for _ in blocks] for blocks in parts]
        for k in range(2):
            columns = slice(k * half, (k + 1) * half)
            total = sums_ref[at, columns]
            for done_ref, blocks in zip(done_refs, part_refs):
                for block, first, end in spans(blocks):
                    total = total + dot(block[0, :, at], done_ref[k, 1, first:end], 0, 0)
            out_ref[:, columns] = total.astype(kind)

    operands = [sums, *done, *(block for blocks in parts for block in blocks)]
    shape = jax.ShapeDtypeStruct((size, 2 * half), kind)
    return local_kernel(body, [shape], row, operands)[0]


def all_of_up(y, factor, blocks, size, width):
    phases, f_width = len(blocks[0]), blocks[0][0].shape[1]
    flat = [block for row in blocks for block in row]
    if f_width % 128 or size % 128:
        result = jnp.zeros((size, width * len(blocks)), jnp.float32)
        for mask, row in enumerate(blocks):
            for phase, block in enumerate(row):
                start = (y[0] ^ mask) * width + phase * f_width
                result = put_at(result, to_f32(block) * factor, start, 1)
        return result

    def put(base, chosen):
        def place_of(step, y):
            result = 0
            for index, (mask, phase) in enumerate(chosen):
                result = jnp.where(step == index, (y[0] ^ mask) * phases + phase, result)
            return result

        def body(y_ref, *refs):
            for index in range(len(chosen)):

                @pl.when(pl.program_id(0) == index)
                def _(ref=refs[index]):
                    refs[-1][...] = to_f32(ref[...]) * factor

        arrays = [blocks[mask][phase] for mask, phase in chosen]
        return pl.pallas_call(
            body,
            out_shape=f32_array(size, width * len(blocks)),
            grid_spec=pltpu.PrefetchScalarGridSpec(
                num_scalar_prefetch=1,
                grid=(len(chosen),),
                in_specs=[IN_VMEM] * len(arrays)
                + [pl.BlockSpec(memory_space=pl.ANY)] * (base is not None),
                out_specs=pl.BlockSpec((size, f_width), lambda step, y: (0, place_of(step, y))),
            ),
            input_output_aliases={} if base is None else {1 + len(arrays): 0},
            compiler_params=pltpu.CompilerParams(vmem_limit_bytes=8 * 2**20),
            cost_estimate=NO_COST,
        )(y, *arrays, *([] if base is None else [base]))

    every = [(mask, phase) for mask in range(len(blocks)) for phase in range(phases)]
    late = [(mask, phase) for mask, phase in every if mask and phase == phases - 1]
    return put(put(None, [pair for pair in every if pair not in late]), late)


def all_of_down(factor, sums, done, parts):
    f_width, features = sums[-1].shape
    half = f_width // 2
    if half % 128:
        total = sums[-1]
        for value, blocks in zip(done, parts):
            both = jnp.concatenate([value[0, 0], value[1, 0]], axis=-1)
            total = total + dot(both, jnp.concatenate(blocks, axis=1)[1], 0, 0)
        return jnp.concatenate([*sums[:-1], total], axis=0) * factor
    steps = 2 * len(sums)

    def body(*refs):
        step, out_ref = pl.program_id(0), refs[-1]
        sum_refs, done_refs = refs[: len(sums)], refs[len(sums) : len(sums) + len(done)]
        block_refs = list(refs[len(sums) + len(done) : -1])
        part_refs = [[block_refs.pop(0) for _ in blocks] for blocks in parts]
        for index in range(steps):

            @pl.when(step == index)
            def _(index=index):
                phase, k = divmod(index, 2)
                total = sum_refs[phase][k * half : (k + 1) * half, :]
                if phase == len(sums) - 1:
                    for done_ref, blocks in zip(done_refs, part_refs):
                        for block, first, end in spans(blocks):
                            total = total + dot(done_ref[k, 0, first:end], block[1], 0, 0)
                out_ref[...] = total * factor

    operands = [*sums, *done, *(block for blocks in parts for block in blocks)]
    return pl.pallas_call(
        body,
        out_shape=f32_array(f_width * len(sums), features),
        grid=(steps,),
        in_specs=[IN_VMEM] * len(operands),
        out_specs=pl.BlockSpec((half, features), lambda step: (step, 0)),
        compiler_params=pltpu.CompilerParams(vmem_limit_bytes=12 * 2**20),
        cost_estimate=NO_COST,
    )(*operands)


def add_inward(place, piece, outer, middle):
    _, _, count, half = piece.shape
    back = 0 if middle is None else middle.shape[1]

    def body(place_ref, piece, outer, *refs):
        place = place_ref[0]
        middle = refs[0] if back else None
        out, inward = refs[-2:]

        def copy(source, size):
            def rows(at):
                out[:, at, :] = source[:, at, :]

            by_rows(size, rows)

        def add(other):
            def rows(at):
                inward[:, at, :] = to_bf16(to_f32(other[:, at, :]) + to_f32(outer[:, at, :]))

            by_rows(count, rows)

        pl.when(place == 0)(lambda: copy(piece.at[0], count))
        pl.when(place == 3)(lambda: copy(piece.at[1], count))
        pl.when(place == 1)(lambda: add(piece.at[1]))
        pl.when(place == 2)(lambda: add(piece.at[0]))
        if back:
            pl.when((place == 1) | (place == 2))(lambda: copy(middle, back))

    shapes = [bf16_array(2, max(count, back), half), bf16_array(2, count, half)]
    operands = [piece, outer] + ([middle] if back else [])
    return local_kernel(body, shapes, place, operands)


def turn_outward(place, piece, outer, middle, following):
    _, _, count, half = piece.shape
    ahead = 0 if following is None else following.shape[2]

    def body(place_ref, piece, outer, middle, *refs):
        place = place_ref[0]
        out, result = refs[-2:]

        def copy(source):
            def rows(at):
                out[:, at, :] = source[:, at, :]

            by_rows(ahead, rows)

        def activate(own):
            def rows(at):
                total = [
                    to_f32(own[k, at, :]) + to_f32(outer[k, at, :]) + to_f32(middle[k, at, :])
                    for k in range(2)
                ]
                active, slope = gelu_parts(total[0])
                for k, value in enumerate((to_bf16(active), to_bf16(total[1] * slope))):
                    result[k, at, :] = value
                    out[k, at, :] = value

            by_rows(count, rows)

        if ahead:
            pl.when(place == 0)(lambda: copy(refs[0].at[1]))
            pl.when(place == 3)(lambda: copy(refs[0].at[0]))
        pl.when(place == 1)(lambda: activate(piece.at[0]))
        pl.when(place == 2)(lambda: activate(piece.at[1]))

    shapes = [bf16_array(2, max(count, ahead), half), bf16_array(2, count, half)]
    operands = [piece, outer, middle] + ([following] if ahead else [])
    return local_kernel(body, shapes, place, operands)


def collect(place, before, outer, outer_2, middle):
    _, count, half = before.shape

    def body(place_ref, before, outer, outer_2, middle, done):
        for index, (low, high) in enumerate(
            [(outer, outer_2), (before, middle), (middle, before), (outer_2, outer)]
        ):

            @pl.when(place_ref[0] == index)
            def _(low=low, high=high):
                def rows(at):
                    done[0, :, at, :] = low[:, at, :]
                    done[1, :, at, :] = high[:, at, :]

                by_rows(count, rows)

    operands = [before, outer, outer_2, middle]
    return local_kernel(body, [bf16_array(2, 2, count, half)], place, operands)[0]


def start_out(place, piece):
    _, _, count, half = piece.shape

    def body(place_ref, piece, out):
        def copy(k):
            def rows(at):
                out[:, at, :] = piece[k, :, at, :]

            by_rows(count, rows)

        pl.when(place_ref[0] == 0)(lambda: copy(1))
        pl.when(place_ref[0] > 0)(lambda: copy(0))

    return local_kernel(body, [bf16_array(2, count, half)], place, [piece])[0]


def line(place, pieces, take, finish):
    pieces = list(pieces)
    piece = take(pieces[0])
    out, before, last = start_out(place, piece), None, None
    for index, upcoming in zip(pieces + [None], pieces[1:] + [None, None]):
        outer, middle = yield out, before
        if index is None:
            outer_2, middle_2 = yield middle, None
        else:
            outer_2, middle_2 = yield add_inward(place, piece, outer, middle)
        if before is not None:
            finish(last, collect(place, before, outer, outer_2, middle))
        if index is not None:
            following = None if upcoming is None else take(upcoming)
            out, before = turn_outward(place, piece, outer_2, middle_2, following)
            piece, last = following, index


def line_swaps(outer, middle):
    arrived = [None, None]
    if outer is not None:
        arrived[0] = lax.ppermute(outer, "col", [(0, 1), (1, 0), (2, 3), (3, 2)])
    if middle is not None:
        arrived[1] = lax.ppermute(middle, "col", [(1, 2), (2, 1)])
    return tuple(arrived)


def per_device(normed, up_weight, down_weight, out_grad):
    n_row, n_col, n_depth = (lax.axis_size(axis) for axis in ("row", "col", "depth"))
    assert n_col == 4
    z, y = lax.axis_index("col"), lax.axis_index("depth")
    width = up_weight.shape[1] // n_depth
    phases = F_PHASES if width % (F_PHASES * 256) == 0 else 1
    f_width = width // phases
    half = f_width // 2
    d_rows = normed.shape[1] // n_depth
    factor = 1.0 / math.sqrt(normed.shape[0] * n_row * n_depth)

    scalars = (
        z.reshape(1),
        y.reshape(1),
        (y * width).reshape(1),
        [((y ^ mask) * d_rows).reshape(1) for mask in range(n_depth)],
    )
    scalars, normed, out_grad, up_weight, down_weight = lax.optimization_barrier(
        (scalars, normed, out_grad, up_weight, down_weight)
    )
    place, layer, first_column, row_at = scalars

    stages = [("depth", mask) for mask in bits(n_depth)]
    stages += [("row", mask) for mask in reversed(bits(n_row))]
    own = normed.shape[0]
    core = stages.pop()
    unit = max(own, (own << len(stages)) // 4)
    early_start = own == unit and half % 128 == 0 and phases == F_PHASES and len(stages) == 2
    early_start = early_start and stages[0][0] == "depth"
    lower = [jnp.stack([normed, out_grad])]
    weights = []
    if early_start:
        upper = [swap(lower[0], *core)]
        weights.append(load(first_column, up_weight, down_weight, 0, f_width, 57))
    else:
        for axis, mask in stages:
            lower += [swap(block, axis, mask) for block in lower]
            if sum(block.shape[1] for block in lower) <= unit:
                lower = [jnp.concatenate(lower, axis=1)]
        upper = [swap(block, *core) for block in lower]
        up = cut_at(up_weight, first_column[0], width, 1)
        down = cut_at(down_weight, first_column[0], width, 0)
        for phase in range(phases):
            at = slice(phase * f_width, (phase + 1) * f_width)
            weights.append((up[:, at], down[at]))

    def gather(slot, value):
        if not early_start or slot not in (2, 4, 5, 7):
            return value
        k = (2, 4, 5, 7).index(slot)
        value, lower[k] = lax.optimization_barrier((value, lower[k]))
        if k == 0:
            lower.extend([swap(lower[0], *stages[0]), swap(lower[0], *stages[1])])
        else:
            upper.append(swap(lower[k], *core))
        if k == 1:
            lower.append(swap(lower[1], *stages[1]))
        return value

    if early_start:
        pieces = [(k, True, True) for k in range(4)]
        order = [(0, 0), (1, 0), (0, 1), (0, 2), (0, 3), (1, 3), (1, 1), (1, 2)]
        order += [(2, 3), (2, 1), (2, 2), (2, 0)]
        order = [(phase,) + pieces[k] for phase, k in order]
    else:
        pieces = [(0, True, False), (0, False, True)] + [(k, True, True) for k in range(1, 4)]
        order = [(0,) + piece for piece in pieces]
        for phase in range(1, phases):
            order += [(phase,) + piece for piece in reversed(pieces)]

    def tokens_of(piece):
        k, has_lower, has_upper = piece
        return [lower[k]] * has_lower + [upper[k]] * has_upper

    def take(index):
        phase, piece = order[index][0], order[index][1:]
        if len(weights) == phase:
            start = phase * f_width
            weights.append(load(first_column, up_weight, down_weight, start, f_width, 8))
        return partials(0, tokens_of(piece), *weights[phase], half)

    outputs, arrived, due = {}, [], []
    seen, kept = [0] * phases, [[] for _ in range(phases)]
    ups, downs, up_blocks = [None] * phases, [None] * phases, [[None] * phases for _ in range(n_depth)]
    slot = 0

    def want(holder, key, slots):
        due.append((slot + slots, holder, key))

    def settle(value, last):
        ready = [(holder, key) for limit, holder, key in due if limit <= last]
        due[:] = [entry for entry in due if entry[0] > last]
        value, arrays = lax.optimization_barrier((value, [holder[key] for holder, key in ready]))
        for (holder, key), array in zip(ready, arrays):
            holder[key] = array
        return value

    def bring(start, total, stage, slots):
        arrived.append([start, swap(total, *stage)])
        want(arrived[-1], 1, slots)

    def send(piece, local):
        k, has_lower, has_upper = piece
        if has_upper:
            bring(k * unit, local[-1], core, 3)
        if not has_lower:
            return
        first = k * unit
        places = [(first, unit)]
        if k == 0:
            small = [own << s for s in range(len(stages)) if own << s < unit]
            places = [(size, size) for size in reversed(small)] + [(0, own)]
        for at, size in places:
            blocks = [local[0][:, at - first : at - first + size]]
            for start, block in arrived:
                if start <= at and at + size <= start + block.shape[1]:
                    blocks.append(block[:, at - start : at - start + size])
            total = None if at == 0 and early_start else sum_of(blocks)
            if at == 0 and early_start:
                outputs["local"] = blocks[0]
            elif at == 0:
                outputs["own"] = total
            else:
                stage = (at // own).bit_length() - 1
                bring(at - (own << stage), total, stages[stage], 6)

    def finish(index, done):
        phase, piece = order[index][0], order[index][1:]
        blocks = tokens_of(piece)
        is_last = phase == phases - 1

        seen[phase] += 1
        kept[phase].append((done, blocks))
        is_end = seen[phase] == len(pieces)
        is_rest = is_last and index >= len(order) - 2
        count = sum(block.shape[1] for _, held in kept[phase] for block in held)
        if not is_rest and (count >= 2 * unit or is_end):
            ups[phase] = gradient(1, ups[phase], *zip(*kept[phase]))
            downs[phase] = gradient(0, downs[phase], *zip(*kept[phase]))
            want(ups, phase, 4)
            want(downs, phase, 6)
            kept[phase].clear()
        if is_end:
            rest = list(zip(*kept[phase])) or [[], []]
            for mask in reversed(range(n_depth)):
                kind = jnp.bfloat16 if mask else jnp.float32
                rows = up_rows(row_at[mask], d_rows, ups[phase], *rest, kind)
                up_blocks[mask][phase] = swap(rows, "depth", mask) if mask else rows
                if mask and not is_last:
                    want(up_blocks[mask], phase, 8)
            if is_last:
                outputs["down"] = all_of_down(factor, downs, *rest)

        sizes = [block.shape[1] for block in blocks]
        outputs[piece] = list(
            outputs_of(0, done, *weights[phase], outputs.get(piece, []), sizes)
        )
        if is_last:
            send(piece, outputs[piece])
        else:
            for part in range(len(sizes)):
                want(outputs[piece], part, 5)

    streams = [
        line(place, range(stream, len(order), STREAMS), take, finish) for stream in range(STREAMS)
    ]
    came = [None] * STREAMS
    payload = None
    while any(streams):
        for which, stream in enumerate(streams):
            if stream is None:
                continue
            slot += 1
            if came[which] is not None:
                came[which] = gather(slot, settle(came[which], slot))
                came[which], _ = lax.optimization_barrier((came[which], payload))
            elif slot == 2:
                payload = gather(slot, payload)
            try:
                payload = lax.optimization_barrier(stream.send(came[which]))
                came[which] = line_swaps(*payload)
            except StopIteration:
                streams[which] = None
    if early_start:
        blocks = [block for start, block in arrived if start == 0]
        outputs["own"] = sum_of([outputs["local"]] + blocks)
    up_grad = all_of_up(layer, factor, up_blocks, d_rows, width)
    return (outputs["own"][0], outputs["own"][1], up_grad, outputs["down"])


def solution(mesh):
    return jax.shard_map(
        per_device,
        mesh=mesh,
        in_specs=(
            P(("depth", "row"), "col"),
            P("col", "row"),
            P("row", "col"),
            P(("depth", "row"), "col"),
        ),
        out_specs=(
            P(("depth", "row"), "col"),
            P(("depth", "row"), "col"),
            P(("col", "depth"), "row"),
            P(("row", "depth"), "col"),
        ),
        check_vma=False,
    )
```

```python
import math

import jax
import jax.numpy as jnp
from jax import lax
from jax.experimental import pallas as pl
from jax.experimental.pallas import tpu as pltpu
from jax.sharding import PartitionSpec as P

F_PHASES = 3
STREAMS = 2
ROWS = 32


def gelu_parts(value):
    coeff = math.sqrt(2.0 / math.pi)
    inner = coeff * (value + 0.044715 * value * value * value)
    tangent = jnp.tanh(inner)
    activated = 0.5 * value * (1.0 + tangent)
    slope = 0.5 * (1.0 + tangent) + 0.5 * value * (1.0 - tangent * tangent) * coeff * (
        1.0 + 3.0 * 0.044715 * value * value
    )
    return (activated, slope)


def dot(left, right, left_dim, right_dim):
    return lax.dot_general(
        left, right, (((left_dim,), (right_dim,)), ((), ())), preferred_element_type=jnp.float32
    )


def to_bf16(value):
    return value.astype(jnp.bfloat16)


def to_f32(value):
    return value.astype(jnp.float32)


def cut_at(array, start, size, dim):
    starts, sizes = [0] * array.ndim, list(array.shape)
    starts[dim], sizes[dim] = start, size
    return lax.dynamic_slice(array, starts, sizes, allow_negative_indices=False)


def put_at(array, part, start, dim):
    starts = [0] * array.ndim
    starts[dim] = start
    return lax.dynamic_update_slice(array, part, starts, allow_negative_indices=False)


def swap(value, axis, mask):
    size = lax.axis_size(axis)
    return lax.ppermute(value, axis, [(i, i ^ mask) for i in range(size)])


def bits(size):
    return [1 << b for b in range(size.bit_length() - 1)]


def by_rows(count, body):
    def step(index, carry):
        body(pl.ds(pl.multiple_of(index * ROWS, ROWS), ROWS))
        return carry

    lax.fori_loop(0, count // ROWS, step, 0)


def bf16_array(*shape):
    return jax.ShapeDtypeStruct(shape, jnp.bfloat16)


def f32_array(*shape):
    return jax.ShapeDtypeStruct(shape, jnp.float32)


NO_COST = pl.CostEstimate(flops=1, bytes_accessed=1, transcendentals=0)
IN_VMEM = pl.BlockSpec(memory_space=pltpu.VMEM)
IN_SMEM = pl.BlockSpec(memory_space=pltpu.SMEM)


def local_kernel(body, out_shapes, scalar, operands, limit=8):
    scalars = [] if scalar is None else [scalar]
    return pl.pallas_call(
        body,
        out_shape=out_shapes,
        in_specs=[IN_SMEM] * len(scalars) + [IN_VMEM] * len(operands),
        out_specs=[IN_VMEM] * len(out_shapes),
        compiler_params=pltpu.CompilerParams(vmem_limit_bytes=limit * 2**20),
        cost_estimate=NO_COST,
    )(*scalars, *operands)


def spans(blocks):
    result, start = [], 0
    for block in blocks:
        result.append((block, start, start + block.shape[1]))
        start += block.shape[1]
    return result


def partials(start, blocks, up, down, half):
    count = sum(block.shape[1] for block in blocks)

    def body(*refs):
        *block_refs, up_ref, down_ref, out_ref = refs
        for k in range(2):
            at = slice(start + k * half, start + (k + 1) * half)
            for block, first, end in spans(block_refs):
                out_ref[k, 0, first:end] = to_bf16(dot(block[0], up_ref[:, at], 1, 0))
                out_ref[k, 1, first:end] = to_bf16(dot(block[1], down_ref[at, :], 1, 1))

    if half % 128:
        part = jnp.concatenate(blocks, axis=1)
        cut = [slice(start + k * half, start + (k + 1) * half) for k in range(2)]
        return to_bf16(
            jnp.stack(
                [
                    jnp.stack([dot(part[0], up[:, at], 1, 0), dot(part[1], down[at], 1, 1)])
                    for at in cut
                ]
            )
        )
    return local_kernel(body, [bf16_array(2, 2, count, half)], None, [*blocks, up, down])[0]


COPIES = 4


def load(column, up_weight, down_weight, start, size, limit):
    features = up_weight.shape[0]
    rows, part = features // COPIES, size // COPIES

    def body(column_ref, up_hbm, down_hbm, up_ref, down_ref, done):
        first = pl.multiple_of(column_ref[0] + start, size)
        copies = []
        for k in range(COPIES):
            at = pl.ds(k * rows, rows)
            copies.append((up_hbm.at[at, pl.ds(first, size)], up_ref.at[at, :]))
            there = pl.ds(pl.multiple_of(first + k * part, part), part)
            copies.append((down_hbm.at[there, :], down_ref.at[pl.ds(k * part, part), :]))
        copies = [
            pltpu.make_async_copy(source, target, done.at[k])
            for k, (source, target) in enumerate(copies)
        ]
        for copy in copies:
            copy.start()
        for copy in copies:
            copy.wait()

    in_place = pl.BlockSpec(memory_space=pl.ANY)
    return pl.pallas_call(
        body,
        out_shape=[bf16_array(features, size), bf16_array(size, features)],
        in_specs=[IN_SMEM, in_place, in_place],
        out_specs=[IN_VMEM] * 2,
        scratch_shapes=[pltpu.SemaphoreType.DMA((2 * COPIES,))],
        compiler_params=pltpu.CompilerParams(vmem_limit_bytes=limit * 2**20),
        cost_estimate=NO_COST,
    )(column, up_weight, down_weight)


def outputs_of(start, done, up, down, so_far, sizes):
    half, features = done.shape[3], up.shape[0]

    def total(done, up, down, before):
        value = list(before)
        for k in range(2):
            at = slice(start + k * half, start + (k + 1) * half)
            value[0] = value[0] + dot(done[k, 0], down[at, :], 1, 0)
            value[1] = value[1] + dot(done[k, 1], up[:, at], 1, 1)
        return value

    def body(done_ref, up_ref, down_ref, *refs):
        outs = refs[-len(sizes) :]
        befores = refs[: -len(sizes)]
        for kind, value in enumerate(total(done_ref, up_ref, down_ref, (0.0, 0.0))):
            first = 0
            for place, size in enumerate(sizes):
                part = value[first : first + size]
                if befores:
                    part = part + to_f32(befores[place][kind])
                outs[place][kind] = to_bf16(part)
                first += size

    if half % 128:
        before = (0.0, 0.0)
        if so_far:
            before = to_f32(jnp.concatenate(so_far, axis=1))
        value = to_bf16(jnp.stack(total(done, up, down, before)))
        return jnp.split(value, [sum(sizes[:k]) for k in range(1, len(sizes))], axis=1)
    shapes = [bf16_array(2, size, features) for size in sizes]
    return local_kernel(body, shapes, None, [done, up, down, *so_far])


def sum_of(blocks):
    if len(blocks) == 1:
        return blocks[0]

    def body(*refs):
        def rows(at):
            for kind in range(2):
                total = to_f32(refs[0][kind, at, :])
                for ref in refs[1:-1]:
                    total = total + to_f32(ref[kind, at, :])
                refs[-1][kind, at, :] = to_bf16(total)

        by_rows(blocks[0].shape[1], rows)

    return local_kernel(body, [bf16_array(*blocks[0].shape)], None, blocks)[0]


def gradient(kind, so_far, done, parts):
    half, features = done[0].shape[3], parts[0][0].shape[2]
    pairs = len(done)
    if half % 128:
        total = 0.0 if so_far is None else so_far
        for value, blocks in zip(done, parts):
            both = jnp.concatenate([value[0, kind], value[1, kind]], axis=-1)
            block = jnp.concatenate(blocks, axis=1)[1 - kind]
            total = total + (dot(block, both, 0, 0) if kind else dot(both, block, 0, 0))
        return total

    def body(*refs):
        done_refs, block_refs, out_ref = refs[:pairs], list(refs[pairs:-1]), refs[-1]
        part_refs = [[block_refs.pop(0) for _ in blocks] for blocks in parts]
        for k in range(2):
            at = slice(k * half, (k + 1) * half)
            total = 0.0
            if so_far is not None:
                total = block_refs[0][:, at] if kind else block_refs[0][at, :]
            for done_ref, blocks in zip(done_refs, part_refs):
                for block, first, end in spans(blocks):
                    value = done_ref[k, kind, first:end]
                    if kind:
                        total = total + dot(block[0], value, 0, 0)
                    else:
                        total = total + dot(value, block[1], 0, 0)
            if kind:
                out_ref[:, at] = total
            else:
                out_ref[at, :] = total

    shape = f32_array(features, 2 * half) if kind else f32_array(2 * half, features)
    operands = [*done, *(block for blocks in parts for block in blocks)]
    operands += [] if so_far is None else [so_far]
    return local_kernel(body, [shape], None, operands, 12)[0]


def up_rows(row, size, sums, done, parts, kind):
    half = sums.shape[1] // 2
    if half % 128:
        total = cut_at(sums, row[0], size, 0)
        for value, blocks in zip(done, parts):
            tokens = cut_at(jnp.concatenate(blocks, axis=1)[0], row[0], size, 1)
            total = total + dot(tokens, jnp.concatenate([value[0, 1], value[1, 1]], axis=-1), 0, 0)
        return total.astype(kind)

    def body(row_ref, sums_ref, *refs):
        at = pl.ds(pl.multiple_of(row_ref[0], size), size)
        out_ref, done_refs = refs[-1], refs[: len(done)]
        block_refs = list(refs[len(done) : -1])
        part_refs = [[block_refs.pop(0) for _ in blocks] for blocks in parts]
        for k in range(2):
            columns = slice(k * half, (k + 1) * half)
            total = sums_ref[at, columns]
            for done_ref, blocks in zip(done_refs, part_refs):
                for block, first, end in spans(blocks):
                    total = total + dot(block[0, :, at], done_ref[k, 1, first:end], 0, 0)
            out_ref[:, columns] = total.astype(kind)

    operands = [sums, *done, *(block for blocks in parts for block in blocks)]
    shape = jax.ShapeDtypeStruct((size, 2 * half), kind)
    return local_kernel(body, [shape], row, operands)[0]


def all_of_up(y, factor, blocks, size, width):
    phases, f_width = len(blocks[0]), blocks[0][0].shape[1]
    flat = [block for row in blocks for block in row]
    if f_width % 128 or size % 128:
        result = jnp.zeros((size, width * len(blocks)), jnp.float32)
        for mask, row in enumerate(blocks):
            for phase, block in enumerate(row):
                start = (y[0] ^ mask) * width + phase * f_width
                result = put_at(result, to_f32(block) * factor, start, 1)
        return result

    def put(base, chosen):
        def place_of(step, y):
            result = 0
            for index, (mask, phase) in enumerate(chosen):
                result = jnp.where(step == index, (y[0] ^ mask) * phases + phase, result)
            return result

        def body(y_ref, *refs):
            for index in range(len(chosen)):

                @pl.when(pl.program_id(0) == index)
                def _(ref=refs[index]):
                    refs[-1][...] = to_f32(ref[...]) * factor

        arrays = [blocks[mask][phase] for mask, phase in chosen]
        return pl.pallas_call(
            body,
            out_shape=f32_array(size, width * len(blocks)),
            grid_spec=pltpu.PrefetchScalarGridSpec(
                num_scalar_prefetch=1,
                grid=(len(chosen),),
                in_specs=[IN_VMEM] * len(arrays)
                + [pl.BlockSpec(memory_space=pl.ANY)] * (base is not None),
                out_specs=pl.BlockSpec((size, f_width), lambda step, y: (0, place_of(step, y))),
            ),
            input_output_aliases={} if base is None else {1 + len(arrays): 0},
            compiler_params=pltpu.CompilerParams(vmem_limit_bytes=8 * 2**20),
            cost_estimate=NO_COST,
        )(y, *arrays, *([] if base is None else [base]))

    every = [(mask, phase) for mask in range(len(blocks)) for phase in range(phases)]
    late = [(mask, phase) for mask, phase in every if mask and phase == phases - 1]
    return put(put(None, [pair for pair in every if pair not in late]), late)


def all_of_down(factor, sums, done, parts):
    f_width, features = sums[-1].shape
    half = f_width // 2
    if half % 128:
        total = sums[-1]
        for value, blocks in zip(done, parts):
            both = jnp.concatenate([value[0, 0], value[1, 0]], axis=-1)
            total = total + dot(both, jnp.concatenate(blocks, axis=1)[1], 0, 0)
        return jnp.concatenate([*sums[:-1], total], axis=0) * factor
    steps = 2 * len(sums)

    def body(*refs):
        step, out_ref = pl.program_id(0), refs[-1]
        sum_refs, done_refs = refs[: len(sums)], refs[len(sums) : len(sums) + len(done)]
        block_refs = list(refs[len(sums) + len(done) : -1])
        part_refs = [[block_refs.pop(0) for _ in blocks] for blocks in parts]
        for index in range(steps):

            @pl.when(step == index)
            def _(index=index):
                phase, k = divmod(index, 2)
                total = sum_refs[phase][k * half : (k + 1) * half, :]
                if phase == len(sums) - 1:
                    for done_ref, blocks in zip(done_refs, part_refs):
                        for block, first, end in spans(blocks):
                            total = total + dot(done_ref[k, 0, first:end], block[1], 0, 0)
                out_ref[...] = total * factor

    operands = [*sums, *done, *(block for blocks in parts for block in blocks)]
    return pl.pallas_call(
        body,
        out_shape=f32_array(f_width * len(sums), features),
        grid=(steps,),
        in_specs=[IN_VMEM] * len(operands),
        out_specs=pl.BlockSpec((half, features), lambda step: (step, 0)),
        compiler_params=pltpu.CompilerParams(vmem_limit_bytes=12 * 2**20),
        cost_estimate=NO_COST,
    )(*operands)


def add_inward(place, piece, outer, middle):
    _, _, count, half = piece.shape
    back = 0 if middle is None else middle.shape[1]

    def body(place_ref, piece, outer, *refs):
        place = place_ref[0]
        middle = refs[0] if back else None
        out, inward = refs[-2:]

        def copy(source, size):
            def rows(at):
                out[:, at, :] = source[:, at, :]

            by_rows(size, rows)

        def add(other):
            def rows(at):
                inward[:, at, :] = to_bf16(to_f32(other[:, at, :]) + to_f32(outer[:, at, :]))

            by_rows(count, rows)

        pl.when(place == 0)(lambda: copy(piece.at[0], count))
        pl.when(place == 3)(lambda: copy(piece.at[1], count))
        pl.when(place == 1)(lambda: add(piece.at[1]))
        pl.when(place == 2)(lambda: add(piece.at[0]))
        if back:
            pl.when((place == 1) | (place == 2))(lambda: copy(middle, back))

    shapes = [bf16_array(2, max(count, back), half), bf16_array(2, count, half)]
    operands = [piece, outer] + ([middle] if back else [])
    return local_kernel(body, shapes, place, operands)


def turn_outward(place, piece, outer, middle, following):
    _, _, count, half = piece.shape
    ahead = 0 if following is None else following.shape[2]

    def body(place_ref, piece, outer, middle, *refs):
        place = place_ref[0]
        out, result = refs[-2:]

        def copy(source):
            def rows(at):
                out[:, at, :] = source[:, at, :]

            by_rows(ahead, rows)

        def activate(own):
            def rows(at):
                total = [
                    to_f32(own[k, at, :]) + to_f32(outer[k, at, :]) + to_f32(middle[k, at, :])
                    for k in range(2)
                ]
                active, slope = gelu_parts(total[0])
                for k, value in enumerate((to_bf16(active), to_bf16(total[1] * slope))):
                    result[k, at, :] = value
                    out[k, at, :] = value

            by_rows(count, rows)

        if ahead:
            pl.when(place == 0)(lambda: copy(refs[0].at[1]))
            pl.when(place == 3)(lambda: copy(refs[0].at[0]))
        pl.when(place == 1)(lambda: activate(piece.at[0]))
        pl.when(place == 2)(lambda: activate(piece.at[1]))

    shapes = [bf16_array(2, max(count, ahead), half), bf16_array(2, count, half)]
    operands = [piece, outer, middle] + ([following] if ahead else [])
    return local_kernel(body, shapes, place, operands)


def collect(place, before, outer, outer_2, middle):
    _, count, half = before.shape

    def body(place_ref, before, outer, outer_2, middle, done):
        for index, (low, high) in enumerate(
            [(outer, outer_2), (before, middle), (middle, before), (outer_2, outer)]
        ):

            @pl.when(place_ref[0] == index)
            def _(low=low, high=high):
                def rows(at):
                    done[0, :, at, :] = low[:, at, :]
                    done[1, :, at, :] = high[:, at, :]

                by_rows(count, rows)

    operands = [before, outer, outer_2, middle]
    return local_kernel(body, [bf16_array(2, 2, count, half)], place, operands)[0]


def start_out(place, piece):
    _, _, count, half = piece.shape

    def body(place_ref, piece, out):
        def copy(k):
            def rows(at):
                out[:, at, :] = piece[k, :, at, :]

            by_rows(count, rows)

        pl.when(place_ref[0] == 0)(lambda: copy(1))
        pl.when(place_ref[0] > 0)(lambda: copy(0))

    return local_kernel(body, [bf16_array(2, count, half)], place, [piece])[0]


def line(place, pieces, take, finish):
    pieces = list(pieces)
    piece = take(pieces[0])
    out, before, last = start_out(place, piece), None, None
    for index, upcoming in zip(pieces + [None], pieces[1:] + [None, None]):
        outer, middle = yield out, before
        if index is None:
            outer_2, middle_2 = yield middle, None
        else:
            outer_2, middle_2 = yield add_inward(place, piece, outer, middle)
        if before is not None:
            finish(last, collect(place, before, outer, outer_2, middle))
        if index is not None:
            following = None if upcoming is None else take(upcoming)
            out, before = turn_outward(place, piece, outer_2, middle_2, following)
            piece, last = following, index


def line_swaps(outer, middle):
    arrived = [None, None]
    if outer is not None:
        arrived[0] = lax.ppermute(outer, "col", [(0, 1), (1, 0), (2, 3), (3, 2)])
    if middle is not None:
        arrived[1] = lax.ppermute(middle, "col", [(1, 2), (2, 1)])
    return tuple(arrived)


def per_device(normed, up_weight, down_weight, out_grad):
    n_row, n_col, n_depth = (lax.axis_size(axis) for axis in ("row", "col", "depth"))
    assert n_col == 4
    z, y = lax.axis_index("col"), lax.axis_index("depth")
    width = up_weight.shape[1] // n_depth
    phases = F_PHASES if width % (F_PHASES * 256) == 0 else 1
    f_width = width // phases
    half = f_width // 2
    d_rows = normed.shape[1] // n_depth
    factor = 1.0 / math.sqrt(normed.shape[0] * n_row * n_depth)

    scalars = (
        z.reshape(1),
        y.reshape(1),
        (y * width).reshape(1),
        [((y ^ mask) * d_rows).reshape(1) for mask in range(n_depth)],
    )
    scalars, normed, out_grad, up_weight, down_weight = lax.optimization_barrier(
        (scalars, normed, out_grad, up_weight, down_weight)
    )
    place, layer, first_column, row_at = scalars

    stages = [("depth", mask) for mask in bits(n_depth)]
    stages += [("row", mask) for mask in reversed(bits(n_row))]
    own = normed.shape[0]
    core = stages.pop()
    unit = max(own, (own << len(stages)) // 4)
    early_start = own == unit and half % 128 == 0 and phases == F_PHASES and len(stages) == 2
    early_start = early_start and stages[0][0] == "depth"
    lower = [jnp.stack([normed, out_grad])]
    weights = []
    if early_start:
        upper = [swap(lower[0], *core)]
        weights.append(load(first_column, up_weight, down_weight, 0, f_width, 57))
    else:
        for axis, mask in stages:
            lower += [swap(block, axis, mask) for block in lower]
            if sum(block.shape[1] for block in lower) <= unit:
                lower = [jnp.concatenate(lower, axis=1)]
        upper = [swap(block, *core) for block in lower]
        up = cut_at(up_weight, first_column[0], width, 1)
        down = cut_at(down_weight, first_column[0], width, 0)
        for phase in range(phases):
            at = slice(phase * f_width, (phase + 1) * f_width)
            weights.append((up[:, at], down[at]))

    def gather(slot, value):
        if not early_start or slot not in (2, 4, 5, 7):
            return value
        k = (2, 4, 5, 7).index(slot)
        value, lower[k] = lax.optimization_barrier((value, lower[k]))
        if k == 0:
            lower.extend([swap(lower[0], *stages[0]), swap(lower[0], *stages[1])])
        else:
            upper.append(swap(lower[k], *core))
        if k == 1:
            lower.append(swap(lower[1], *stages[1]))
        return value

    if early_start:
        pieces = [(k, True, True) for k in range(4)]
        order = [(0, 0), (1, 0), (0, 1), (0, 2), (0, 3), (1, 3), (1, 1), (1, 2)]
        order += [(2, 0), (2, 3), (2, 1), (2, 2)]
        order = [(phase,) + pieces[k] for phase, k in order]
    else:
        pieces = [(0, True, False), (0, False, True)] + [(k, True, True) for k in range(1, 4)]
        order = [(0,) + piece for piece in pieces]
        for phase in range(1, phases):
            order += [(phase,) + piece for piece in reversed(pieces)]

    def tokens_of(piece):
        k, has_lower, has_upper = piece
        return [lower[k]] * has_lower + [upper[k]] * has_upper

    def take(index):
        phase, piece = order[index][0], order[index][1:]
        if len(weights) == phase:
            start = phase * f_width
            weights.append(load(first_column, up_weight, down_weight, start, f_width, 8))
        return partials(0, tokens_of(piece), *weights[phase], half)

    outputs, arrived, due = {}, [], []
    seen, kept = [0] * phases, [[] for _ in range(phases)]
    ups, downs, up_blocks = [None] * phases, [None] * phases, [[None] * phases for _ in range(n_depth)]
    slot = 0

    def want(holder, key, slots):
        due.append((slot + slots, holder, key))

    def settle(value, last):
        ready = [(holder, key) for limit, holder, key in due if limit <= last]
        due[:] = [entry for entry in due if entry[0] > last]
        value, arrays = lax.optimization_barrier((value, [holder[key] for holder, key in ready]))
        for (holder, key), array in zip(ready, arrays):
            holder[key] = array
        return value

    def bring(start, total, stage, slots):
        arrived.append([start, swap(total, *stage)])
        want(arrived[-1], 1, slots)

    def send(piece, local):
        k, has_lower, has_upper = piece
        if has_upper:
            bring(k * unit, local[-1], core, 3)
        if not has_lower:
            return
        first = k * unit
        places = [(first, unit)]
        if k == 0:
            small = [own << s for s in range(len(stages)) if own << s < unit]
            places = [(size, size) for size in reversed(small)] + [(0, own)]
        for at, size in places:
            blocks = [local[0][:, at - first : at - first + size]]
            for start, block in arrived:
                if start <= at and at + size <= start + block.shape[1]:
                    blocks.append(block[:, at - start : at - start + size])
            total = None if at == 0 and early_start else sum_of(blocks)
            if at == 0 and early_start:
                outputs["local"] = blocks[0]
            elif at == 0:
                outputs["own"] = total
            else:
                stage = (at // own).bit_length() - 1
                bring(at - (own << stage), total, stages[stage], 5)

    def finish(index, done):
        phase, piece = order[index][0], order[index][1:]
        blocks = tokens_of(piece)
        is_last = phase == phases - 1

        seen[phase] += 1
        kept[phase].append((done, blocks))
        is_end = seen[phase] == len(pieces)
        is_rest = is_last and index >= len(order) - 2
        count = sum(block.shape[1] for _, held in kept[phase] for block in held)
        if not is_rest and (count >= 2 * unit or is_end):
            ups[phase] = gradient(1, ups[phase], *zip(*kept[phase]))
            downs[phase] = gradient(0, downs[phase], *zip(*kept[phase]))
            want(ups, phase, 4)
            want(downs, phase, 5)
            kept[phase].clear()
        if is_end:
            rest = list(zip(*kept[phase])) or [[], []]
            for mask in reversed(range(n_depth)):
                kind = jnp.bfloat16 if mask else jnp.float32
                rows = up_rows(row_at[mask], d_rows, ups[phase], *rest, kind)
                up_blocks[mask][phase] = swap(rows, "depth", mask) if mask else rows
                if mask and not is_last:
                    want(up_blocks[mask], phase, 7)
            if is_last:
                outputs["down"] = all_of_down(factor, downs, *rest)

        sizes = [block.shape[1] for block in blocks]
        outputs[piece] = list(
            outputs_of(0, done, *weights[phase], outputs.get(piece, []), sizes)
        )
        if is_last:
            send(piece, outputs[piece])
        else:
            for part in range(len(sizes)):
                want(outputs[piece], part, 5)

    streams = [
        line(place, range(stream, len(order), STREAMS), take, finish) for stream in range(STREAMS)
    ]
    came = [None] * STREAMS
    payload = None
    while any(streams):
        for which, stream in enumerate(streams):
            if stream is None:
                continue
            slot += 1
            if came[which] is not None:
                came[which] = gather(slot, settle(came[which], slot))
                came[which], _ = lax.optimization_barrier((came[which], payload))
            elif slot == 2:
                payload = gather(slot, payload)
            try:
                payload = lax.optimization_barrier(stream.send(came[which]))
                came[which] = line_swaps(*payload)
            except StopIteration:
                streams[which] = None
    if early_start:
        blocks = [block for start, block in arrived if start == 0]
        outputs["own"] = sum_of([outputs["local"]] + blocks)
    up_grad = all_of_up(layer, factor, up_blocks, d_rows, width)
    return (outputs["own"][0], outputs["own"][1], up_grad, outputs["down"])


def solution(mesh):
    return jax.shard_map(
        per_device,
        mesh=mesh,
        in_specs=(
            P(("depth", "row"), "col"),
            P("col", "row"),
            P("row", "col"),
            P(("depth", "row"), "col"),
        ),
        out_specs=(
            P(("depth", "row"), "col"),
            P(("depth", "row"), "col"),
            P(("col", "depth"), "row"),
            P(("row", "depth"), "col"),
        ),
        check_vma=False,
    )
```

```python
import math

import jax
import jax.numpy as jnp
from jax import lax
from jax.experimental import pallas as pl
from jax.experimental.pallas import tpu as pltpu
from jax.sharding import PartitionSpec as P

F_PHASES = 3
STREAMS = 2
ROWS = 32


def gelu_parts(value):
    coeff = math.sqrt(2.0 / math.pi)
    inner = coeff * (value + 0.044715 * value * value * value)
    tangent = jnp.tanh(inner)
    activated = 0.5 * value * (1.0 + tangent)
    slope = 0.5 * (1.0 + tangent) + 0.5 * value * (1.0 - tangent * tangent) * coeff * (
        1.0 + 3.0 * 0.044715 * value * value
    )
    return (activated, slope)


def dot(left, right, left_dim, right_dim):
    return lax.dot_general(
        left, right, (((left_dim,), (right_dim,)), ((), ())), preferred_element_type=jnp.float32
    )


def to_bf16(value):
    return value.astype(jnp.bfloat16)


def to_f32(value):
    return value.astype(jnp.float32)


def cut_at(array, start, size, dim):
    starts, sizes = [0] * array.ndim, list(array.shape)
    starts[dim], sizes[dim] = start, size
    return lax.dynamic_slice(array, starts, sizes, allow_negative_indices=False)


def put_at(array, part, start, dim):
    starts = [0] * array.ndim
    starts[dim] = start
    return lax.dynamic_update_slice(array, part, starts, allow_negative_indices=False)


def swap(value, axis, mask):
    size = lax.axis_size(axis)
    return lax.ppermute(value, axis, [(i, i ^ mask) for i in range(size)])


def bits(size):
    return [1 << b for b in range(size.bit_length() - 1)]


def by_rows(count, body):
    def step(index, carry):
        body(pl.ds(pl.multiple_of(index * ROWS, ROWS), ROWS))
        return carry

    lax.fori_loop(0, count // ROWS, step, 0)


def bf16_array(*shape):
    return jax.ShapeDtypeStruct(shape, jnp.bfloat16)


def f32_array(*shape):
    return jax.ShapeDtypeStruct(shape, jnp.float32)


NO_COST = pl.CostEstimate(flops=1, bytes_accessed=1, transcendentals=0)
IN_VMEM = pl.BlockSpec(memory_space=pltpu.VMEM)
IN_SMEM = pl.BlockSpec(memory_space=pltpu.SMEM)


def local_kernel(body, out_shapes, scalar, operands, limit=8):
    scalars = [] if scalar is None else [scalar]
    return pl.pallas_call(
        body,
        out_shape=out_shapes,
        in_specs=[IN_SMEM] * len(scalars) + [IN_VMEM] * len(operands),
        out_specs=[IN_VMEM] * len(out_shapes),
        compiler_params=pltpu.CompilerParams(vmem_limit_bytes=limit * 2**20),
        cost_estimate=NO_COST,
    )(*scalars, *operands)


def spans(blocks):
    result, start = [], 0
    for block in blocks:
        result.append((block, start, start + block.shape[1]))
        start += block.shape[1]
    return result


def partials(start, blocks, up, down, half):
    count = sum(block.shape[1] for block in blocks)

    def body(*refs):
        *block_refs, up_ref, down_ref, out_ref = refs
        for k in range(2):
            at = slice(start + k * half, start + (k + 1) * half)
            for block, first, end in spans(block_refs):
                out_ref[k, 0, first:end] = to_bf16(dot(block[0], up_ref[:, at], 1, 0))
                out_ref[k, 1, first:end] = to_bf16(dot(block[1], down_ref[at, :], 1, 1))

    if half % 128:
        part = jnp.concatenate(blocks, axis=1)
        cut = [slice(start + k * half, start + (k + 1) * half) for k in range(2)]
        return to_bf16(
            jnp.stack(
                [
                    jnp.stack([dot(part[0], up[:, at], 1, 0), dot(part[1], down[at], 1, 1)])
                    for at in cut
                ]
            )
        )
    return local_kernel(body, [bf16_array(2, 2, count, half)], None, [*blocks, up, down])[0]


COPIES = 4


def load(column, up_weight, down_weight, start, size, limit):
    features = up_weight.shape[0]
    rows, part = features // COPIES, size // COPIES

    def body(column_ref, up_hbm, down_hbm, up_ref, down_ref, done):
        first = pl.multiple_of(column_ref[0] + start, size)
        copies = []
        for k in range(COPIES):
            at = pl.ds(k * rows, rows)
            copies.append((up_hbm.at[at, pl.ds(first, size)], up_ref.at[at, :]))
            there = pl.ds(pl.multiple_of(first + k * part, part), part)
            copies.append((down_hbm.at[there, :], down_ref.at[pl.ds(k * part, part), :]))
        copies = [
            pltpu.make_async_copy(source, target, done.at[k])
            for k, (source, target) in enumerate(copies)
        ]
        for copy in copies:
            copy.start()
        for copy in copies:
            copy.wait()

    in_place = pl.BlockSpec(memory_space=pl.ANY)
    return pl.pallas_call(
        body,
        out_shape=[bf16_array(features, size), bf16_array(size, features)],
        in_specs=[IN_SMEM, in_place, in_place],
        out_specs=[IN_VMEM] * 2,
        scratch_shapes=[pltpu.SemaphoreType.DMA((2 * COPIES,))],
        compiler_params=pltpu.CompilerParams(vmem_limit_bytes=limit * 2**20),
        cost_estimate=NO_COST,
    )(column, up_weight, down_weight)


def outputs_of(start, done, up, down, so_far, sizes):
    half, features = done.shape[3], up.shape[0]

    def total(done, up, down, before):
        value = list(before)
        for k in range(2):
            at = slice(start + k * half, start + (k + 1) * half)
            value[0] = value[0] + dot(done[k, 0], down[at, :], 1, 0)
            value[1] = value[1] + dot(done[k, 1], up[:, at], 1, 1)
        return value

    def body(done_ref, up_ref, down_ref, *refs):
        outs = refs[-len(sizes) :]
        befores = refs[: -len(sizes)]
        for kind, value in enumerate(total(done_ref, up_ref, down_ref, (0.0, 0.0))):
            first = 0
            for place, size in enumerate(sizes):
                part = value[first : first + size]
                if befores:
                    part = part + to_f32(befores[place][kind])
                outs[place][kind] = to_bf16(part)
                first += size

    if half % 128:
        before = (0.0, 0.0)
        if so_far:
            before = to_f32(jnp.concatenate(so_far, axis=1))
        value = to_bf16(jnp.stack(total(done, up, down, before)))
        return jnp.split(value, [sum(sizes[:k]) for k in range(1, len(sizes))], axis=1)
    shapes = [bf16_array(2, size, features) for size in sizes]
    return local_kernel(body, shapes, None, [done, up, down, *so_far])


def sum_of(blocks):
    if len(blocks) == 1:
        return blocks[0]

    def body(*refs):
        def rows(at):
            for kind in range(2):
                total = to_f32(refs[0][kind, at, :])
                for ref in refs[1:-1]:
                    total = total + to_f32(ref[kind, at, :])
                refs[-1][kind, at, :] = to_bf16(total)

        by_rows(blocks[0].shape[1], rows)

    return local_kernel(body, [bf16_array(*blocks[0].shape)], None, blocks)[0]


def gradient(kind, so_far, done, parts):
    half, features = done[0].shape[3], parts[0][0].shape[2]
    pairs = len(done)
    if half % 128:
        total = 0.0 if so_far is None else so_far
        for value, blocks in zip(done, parts):
            both = jnp.concatenate([value[0, kind], value[1, kind]], axis=-1)
            block = jnp.concatenate(blocks, axis=1)[1 - kind]
            total = total + (dot(block, both, 0, 0) if kind else dot(both, block, 0, 0))
        return total

    def body(*refs):
        done_refs, block_refs, out_ref = refs[:pairs], list(refs[pairs:-1]), refs[-1]
        part_refs = [[block_refs.pop(0) for _ in blocks] for blocks in parts]
        for k in range(2):
            at = slice(k * half, (k + 1) * half)
            total = 0.0
            if so_far is not None:
                total = block_refs[0][:, at] if kind else block_refs[0][at, :]
            for done_ref, blocks in zip(done_refs, part_refs):
                for block, first, end in spans(blocks):
                    value = done_ref[k, kind, first:end]
                    if kind:
                        total = total + dot(block[0], value, 0, 0)
                    else:
                        total = total + dot(value, block[1], 0, 0)
            if kind:
                out_ref[:, at] = total
            else:
                out_ref[at, :] = total

    shape = f32_array(features, 2 * half) if kind else f32_array(2 * half, features)
    operands = [*done, *(block for blocks in parts for block in blocks)]
    operands += [] if so_far is None else [so_far]
    return local_kernel(body, [shape], None, operands, 12)[0]


def up_rows(row, size, sums, done, parts, kind):
    half = sums.shape[1] // 2
    if half % 128:
        total = cut_at(sums, row[0], size, 0)
        for value, blocks in zip(done, parts):
            tokens = cut_at(jnp.concatenate(blocks, axis=1)[0], row[0], size, 1)
            total = total + dot(tokens, jnp.concatenate([value[0, 1], value[1, 1]], axis=-1), 0, 0)
        return total.astype(kind)

    def body(row_ref, sums_ref, *refs):
        at = pl.ds(pl.multiple_of(row_ref[0], size), size)
        out_ref, done_refs = refs[-1], refs[: len(done)]
        block_refs = list(refs[len(done) : -1])
        part_refs = [[block_refs.pop(0) for _ in blocks] for blocks in parts]
        for k in range(2):
            columns = slice(k * half, (k + 1) * half)
            total = sums_ref[at, columns]
            for done_ref, blocks in zip(done_refs, part_refs):
                for block, first, end in spans(blocks):
                    total = total + dot(block[0, :, at], done_ref[k, 1, first:end], 0, 0)
            out_ref[:, columns] = total.astype(kind)

    operands = [sums, *done, *(block for blocks in parts for block in blocks)]
    shape = jax.ShapeDtypeStruct((size, 2 * half), kind)
    return local_kernel(body, [shape], row, operands)[0]


def all_of_up(y, factor, blocks, size, width):
    phases, f_width = len(blocks[0]), blocks[0][0].shape[1]
    flat = [block for row in blocks for block in row]
    if f_width % 128 or size % 128:
        result = jnp.zeros((size, width * len(blocks)), jnp.float32)
        for mask, row in enumerate(blocks):
            for phase, block in enumerate(row):
                start = (y[0] ^ mask) * width + phase * f_width
                result = put_at(result, to_f32(block) * factor, start, 1)
        return result

    def put(base, chosen):
        def place_of(step, y):
            result = 0
            for index, (mask, phase) in enumerate(chosen):
                result = jnp.where(step == index, (y[0] ^ mask) * phases + phase, result)
            return result

        def body(y_ref, *refs):
            for index in range(len(chosen)):

                @pl.when(pl.program_id(0) == index)
                def _(ref=refs[index]):
                    refs[-1][...] = to_f32(ref[...]) * factor

        arrays = [blocks[mask][phase] for mask, phase in chosen]
        return pl.pallas_call(
            body,
            out_shape=f32_array(size, width * len(blocks)),
            grid_spec=pltpu.PrefetchScalarGridSpec(
                num_scalar_prefetch=1,
                grid=(len(chosen),),
                in_specs=[IN_VMEM] * len(arrays)
                + [pl.BlockSpec(memory_space=pl.ANY)] * (base is not None),
                out_specs=pl.BlockSpec((size, f_width), lambda step, y: (0, place_of(step, y))),
            ),
            input_output_aliases={} if base is None else {1 + len(arrays): 0},
            compiler_params=pltpu.CompilerParams(vmem_limit_bytes=8 * 2**20),
            cost_estimate=NO_COST,
        )(y, *arrays, *([] if base is None else [base]))

    every = [(mask, phase) for mask in range(len(blocks)) for phase in range(phases)]
    late = [(mask, phase) for mask, phase in every if mask and phase == phases - 1]
    return put(put(None, [pair for pair in every if pair not in late]), late)


def all_of_down(factor, sums, done, parts):
    f_width, features = sums[-1].shape
    half = f_width // 2
    if half % 128:
        total = sums[-1]
        for value, blocks in zip(done, parts):
            both = jnp.concatenate([value[0, 0], value[1, 0]], axis=-1)
            total = total + dot(both, jnp.concatenate(blocks, axis=1)[1], 0, 0)
        return jnp.concatenate([*sums[:-1], total], axis=0) * factor
    steps = 2 * len(sums)

    def body(*refs):
        step, out_ref = pl.program_id(0), refs[-1]
        sum_refs, done_refs = refs[: len(sums)], refs[len(sums) : len(sums) + len(done)]
        block_refs = list(refs[len(sums) + len(done) : -1])
        part_refs = [[block_refs.pop(0) for _ in blocks] for blocks in parts]
        for index in range(steps):

            @pl.when(step == index)
            def _(index=index):
                phase, k = divmod(index, 2)
                total = sum_refs[phase][k * half : (k + 1) * half, :]
                if phase == len(sums) - 1:
                    for done_ref, blocks in zip(done_refs, part_refs):
                        for block, first, end in spans(blocks):
                            total = total + dot(done_ref[k, 0, first:end], block[1], 0, 0)
                out_ref[...] = total * factor

    operands = [*sums, *done, *(block for blocks in parts for block in blocks)]
    return pl.pallas_call(
        body,
        out_shape=f32_array(f_width * len(sums), features),
        grid=(steps,),
        in_specs=[IN_VMEM] * len(operands),
        out_specs=pl.BlockSpec((half, features), lambda step: (step, 0)),
        compiler_params=pltpu.CompilerParams(vmem_limit_bytes=12 * 2**20),
        cost_estimate=NO_COST,
    )(*operands)


def add_inward(place, piece, outer, middle):
    _, _, count, half = piece.shape
    back = 0 if middle is None else middle.shape[1]

    def body(place_ref, piece, outer, *refs):
        place = place_ref[0]
        middle = refs[0] if back else None
        out, inward = refs[-2:]

        def copy(source, size):
            def rows(at):
                out[:, at, :] = source[:, at, :]

            by_rows(size, rows)

        def add(other):
            def rows(at):
                inward[:, at, :] = to_bf16(to_f32(other[:, at, :]) + to_f32(outer[:, at, :]))

            by_rows(count, rows)

        pl.when(place == 0)(lambda: copy(piece.at[0], count))
        pl.when(place == 3)(lambda: copy(piece.at[1], count))
        pl.when(place == 1)(lambda: add(piece.at[1]))
        pl.when(place == 2)(lambda: add(piece.at[0]))
        if back:
            pl.when((place == 1) | (place == 2))(lambda: copy(middle, back))

    shapes = [bf16_array(2, max(count, back), half), bf16_array(2, count, half)]
    operands = [piece, outer] + ([middle] if back else [])
    return local_kernel(body, shapes, place, operands)


def turn_outward(place, piece, outer, middle, following):
    _, _, count, half = piece.shape
    ahead = 0 if following is None else following.shape[2]

    def body(place_ref, piece, outer, middle, *refs):
        place = place_ref[0]
        out, result = refs[-2:]

        def copy(source):
            def rows(at):
                out[:, at, :] = source[:, at, :]

            by_rows(ahead, rows)

        def activate(own):
            def rows(at):
                total = [
                    to_f32(own[k, at, :]) + to_f32(outer[k, at, :]) + to_f32(middle[k, at, :])
                    for k in range(2)
                ]
                active, slope = gelu_parts(total[0])
                for k, value in enumerate((to_bf16(active), to_bf16(total[1] * slope))):
                    result[k, at, :] = value
                    out[k, at, :] = value

            by_rows(count, rows)

        if ahead:
            pl.when(place == 0)(lambda: copy(refs[0].at[1]))
            pl.when(place == 3)(lambda: copy(refs[0].at[0]))
        pl.when(place == 1)(lambda: activate(piece.at[0]))
        pl.when(place == 2)(lambda: activate(piece.at[1]))

    shapes = [bf16_array(2, max(count, ahead), half), bf16_array(2, count, half)]
    operands = [piece, outer, middle] + ([following] if ahead else [])
    return local_kernel(body, shapes, place, operands)


def collect(place, before, outer, outer_2, middle):
    _, count, half = before.shape

    def body(place_ref, before, outer, outer_2, middle, done):
        for index, (low, high) in enumerate(
            [(outer, outer_2), (before, middle), (middle, before), (outer_2, outer)]
        ):

            @pl.when(place_ref[0] == index)
            def _(low=low, high=high):
                def rows(at):
                    done[0, :, at, :] = low[:, at, :]
                    done[1, :, at, :] = high[:, at, :]

                by_rows(count, rows)

    operands = [before, outer, outer_2, middle]
    return local_kernel(body, [bf16_array(2, 2, count, half)], place, operands)[0]


def start_out(place, piece):
    _, _, count, half = piece.shape

    def body(place_ref, piece, out):
        def copy(k):
            def rows(at):
                out[:, at, :] = piece[k, :, at, :]

            by_rows(count, rows)

        pl.when(place_ref[0] == 0)(lambda: copy(1))
        pl.when(place_ref[0] > 0)(lambda: copy(0))

    return local_kernel(body, [bf16_array(2, count, half)], place, [piece])[0]


def line(place, pieces, take, finish):
    pieces = list(pieces)
    piece = take(pieces[0])
    out, before, last = start_out(place, piece), None, None
    for index, upcoming in zip(pieces + [None], pieces[1:] + [None, None]):
        outer, middle = yield out, before
        if index is None:
            outer_2, middle_2 = yield middle, None
        else:
            outer_2, middle_2 = yield add_inward(place, piece, outer, middle)
        if before is not None:
            finish(last, collect(place, before, outer, outer_2, middle))
        if index is not None:
            following = None if upcoming is None else take(upcoming)
            out, before = turn_outward(place, piece, outer_2, middle_2, following)
            piece, last = following, index


def line_swaps(outer, middle):
    arrived = [None, None]
    if outer is not None:
        arrived[0] = lax.ppermute(outer, "col", [(0, 1), (1, 0), (2, 3), (3, 2)])
    if middle is not None:
        arrived[1] = lax.ppermute(middle, "col", [(1, 2), (2, 1)])
    return tuple(arrived)


def per_device(normed, up_weight, down_weight, out_grad):
    n_row, n_col, n_depth = (lax.axis_size(axis) for axis in ("row", "col", "depth"))
    assert n_col == 4
    z, y = lax.axis_index("col"), lax.axis_index("depth")
    width = up_weight.shape[1] // n_depth
    phases = F_PHASES if width % (F_PHASES * 256) == 0 else 1
    f_width = width // phases
    half = f_width // 2
    d_rows = normed.shape[1] // n_depth
    factor = 1.0 / math.sqrt(normed.shape[0] * n_row * n_depth)

    scalars = (
        z.reshape(1),
        y.reshape(1),
        (y * width).reshape(1),
        [((y ^ mask) * d_rows).reshape(1) for mask in range(n_depth)],
    )
    scalars, normed, out_grad, up_weight, down_weight = lax.optimization_barrier(
        (scalars, normed, out_grad, up_weight, down_weight)
    )
    place, layer, first_column, row_at = scalars

    stages = [("depth", mask) for mask in bits(n_depth)]
    stages += [("row", mask) for mask in reversed(bits(n_row))]
    own = normed.shape[0]
    core = stages.pop()
    unit = max(own, (own << len(stages)) // 4)
    early_start = own == unit and half % 128 == 0 and phases == F_PHASES and len(stages) == 2
    early_start = early_start and stages[0][0] == "depth"
    lower = [jnp.stack([normed, out_grad])]
    weights = []
    if early_start:
        upper = [swap(lower[0], *core)]
        weights.append(load(first_column, up_weight, down_weight, 0, f_width, 57))
    else:
        for axis, mask in stages:
            lower += [swap(block, axis, mask) for block in lower]
            if sum(block.shape[1] for block in lower) <= unit:
                lower = [jnp.concatenate(lower, axis=1)]
        upper = [swap(block, *core) for block in lower]
        up = cut_at(up_weight, first_column[0], width, 1)
        down = cut_at(down_weight, first_column[0], width, 0)
        for phase in range(phases):
            at = slice(phase * f_width, (phase + 1) * f_width)
            weights.append((up[:, at], down[at]))

    def gather(slot, value):
        if not early_start or slot not in (2, 4, 5, 7):
            return value
        k = (2, 4, 5, 7).index(slot)
        value, lower[k] = lax.optimization_barrier((value, lower[k]))
        if k == 0:
            lower.extend([swap(lower[0], *stages[0]), swap(lower[0], *stages[1])])
        else:
            upper.append(swap(lower[k], *core))
        if k == 1:
            lower.append(swap(lower[1], *stages[1]))
        return value

    if early_start:
        pieces = [(k, True, True) for k in range(4)]
        order = [(0, 0), (1, 0), (0, 1), (0, 2), (0, 3), (1, 3), (1, 1), (1, 2)]
        order += [(2, 3), (2, 1), (2, 2), (2, 0)]
        order = [(phase,) + pieces[k] for phase, k in order]
    else:
        pieces = [(0, True, False), (0, False, True)] + [(k, True, True) for k in range(1, 4)]
        order = [(0,) + piece for piece in pieces]
        for phase in range(1, phases):
            order += [(phase,) + piece for piece in reversed(pieces)]

    def tokens_of(piece):
        k, has_lower, has_upper = piece
        return [lower[k]] * has_lower + [upper[k]] * has_upper

    def take(index):
        phase, piece = order[index][0], order[index][1:]
        if len(weights) == phase:
            start = phase * f_width
            weights.append(load(first_column, up_weight, down_weight, start, f_width, 8))
        return partials(0, tokens_of(piece), *weights[phase], half)

    outputs, arrived, due = {}, [], []
    seen, kept = [0] * phases, [[] for _ in range(phases)]
    ups, downs, up_blocks = [None] * phases, [None] * phases, [[None] * phases for _ in range(n_depth)]
    slot = 0

    def want(holder, key, slots):
        due.append((slot + slots, holder, key))

    def settle(value, last):
        ready = [(holder, key) for limit, holder, key in due if limit <= last]
        due[:] = [entry for entry in due if entry[0] > last]
        value, arrays = lax.optimization_barrier((value, [holder[key] for holder, key in ready]))
        for (holder, key), array in zip(ready, arrays):
            holder[key] = array
        return value

    def bring(start, total, stage, slots):
        arrived.append([start, swap(total, *stage)])
        want(arrived[-1], 1, slots)

    def send(piece, local):
        k, has_lower, has_upper = piece
        if has_upper:
            bring(k * unit, local[-1], core, 3)
        if not has_lower:
            return
        first = k * unit
        places = [(first, unit)]
        if k == 0:
            small = [own << s for s in range(len(stages)) if own << s < unit]
            places = [(size, size) for size in reversed(small)] + [(0, own)]
        for at, size in places:
            blocks = [local[0][:, at - first : at - first + size]]
            for start, block in arrived:
                if start <= at and at + size <= start + block.shape[1]:
                    blocks.append(block[:, at - start : at - start + size])
            total = None if at == 0 and early_start else sum_of(blocks)
            if at == 0 and early_start:
                outputs["local"] = blocks[0]
            elif at == 0:
                outputs["own"] = total
            else:
                stage = (at // own).bit_length() - 1
                bring(at - (own << stage), total, stages[stage], 6 if k == 1 else 6)

    def finish(index, done):
        phase, piece = order[index][0], order[index][1:]
        blocks = tokens_of(piece)
        is_last = phase == phases - 1

        seen[phase] += 1
        kept[phase].append((done, blocks))
        is_end = seen[phase] == len(pieces)
        is_rest = is_last and index >= len(order) - 2
        count = sum(block.shape[1] for _, held in kept[phase] for block in held)
        if not is_rest and (count >= 2 * unit or is_end):
            ups[phase] = gradient(1, ups[phase], *zip(*kept[phase]))
            downs[phase] = gradient(0, downs[phase], *zip(*kept[phase]))
            want(ups, phase, 5)
            want(downs, phase, 7)
            kept[phase].clear()
        if is_end:
            rest = list(zip(*kept[phase])) or [[], []]
            for mask in reversed(range(n_depth)):
                kind = jnp.bfloat16 if mask else jnp.float32
                rows = up_rows(row_at[mask], d_rows, ups[phase], *rest, kind)
                up_blocks[mask][phase] = swap(rows, "depth", mask) if mask else rows
                if mask and not is_last:
                    want(up_blocks[mask], phase, 9)
            if is_last:
                outputs["down"] = all_of_down(factor, downs, *rest)

        sizes = [block.shape[1] for block in blocks]
        outputs[piece] = list(
            outputs_of(0, done, *weights[phase], outputs.get(piece, []), sizes)
        )
        if is_last:
            send(piece, outputs[piece])
        else:
            for part in range(len(sizes)):
                want(outputs[piece], part, 6)

    streams = [
        line(place, range(stream, len(order), STREAMS), take, finish) for stream in range(STREAMS)
    ]
    came = [None] * STREAMS
    payload = None
    while any(streams):
        for which, stream in enumerate(streams):
            if stream is None:
                continue
            slot += 1
            if came[which] is not None:
                came[which] = gather(slot, settle(came[which], slot))
                came[which], _ = lax.optimization_barrier((came[which], payload))
            elif slot == 2:
                payload = gather(slot, payload)
            try:
                payload = lax.optimization_barrier(stream.send(came[which]))
                came[which] = line_swaps(*payload)
            except StopIteration:
                streams[which] = None
    if early_start:
        blocks = [block for start, block in arrived if start == 0]
        outputs["own"] = sum_of([outputs["local"]] + blocks)
    up_grad = all_of_up(layer, factor, up_blocks, d_rows, width)
    return (outputs["own"][0], outputs["own"][1], up_grad, outputs["down"])


def solution(mesh):
    return jax.shard_map(
        per_device,
        mesh=mesh,
        in_specs=(
            P(("depth", "row"), "col"),
            P("col", "row"),
            P("row", "col"),
            P(("depth", "row"), "col"),
        ),
        out_specs=(
            P(("depth", "row"), "col"),
            P(("depth", "row"), "col"),
            P(("col", "depth"), "row"),
            P(("row", "depth"), "col"),
        ),
        check_vma=False,
    )
```
